32 devices in a mesh: grp: 2 (over y), hid: 4 (over z), ex: 4 (over x, core).
Axes of the slice: x: 2, y: 2, z: 4, core: 2. Of those that a mesh axis runs over, the one named last changes fastest.
Arguments:
- in_acts: bfloat16 [32768, 4096], P(('grp', 'ex'), 'hid'), parts along dimension 0, may hold values from -6 to 6
- out_grad: bfloat16 [32768, 14336], P(('grp', 'ex'), 'hid'), parts along dimension 0, may hold values from -6 to 6
- proj_in: bfloat16 [4096, 64], P('hid'), may hold values from -0.09375 to 0.09375
- proj_out: bfloat16 [14336, 64], P('hid'), may hold values from -0.046875 to 0.046875
- token_ids: int32 [128, 256], P(('grp', 'ex')), parts along dimension 0, may hold values from 0 to 128255
- token_weight: float32 [128256], replicated, may hold values from 0.25 to 4
- query_ids: int32 [64], P('grp'), parts along dimension 0, may hold values from 0 to 63
Outputs:
- seq_grads: float32 [128, 64, 64], P(('grp', 'ex'), 'hid'), parts along dimension 0
- scores: float32 [64, 64], P('grp', 'ex'), parts along dimension 0
The draws below stay inside these ranges and needn't reach their ends.
There are 2 independent parts, one for each index of `grp`. The reference program is written for one: setup_inputs(seed, part) draws one part's arguments, and reference() takes and returns one part's arrays. A program takes and returns all parts, laid end to end along the dimension named above; an argument that names none is the same for every part. Nothing has to cross between parts.
Inputs may be any that keep to these rules, and one draw needn't show every extreme that they name: `query_ids`: indices of training sequences of this part.
All inputs are finite; a program needn't handle non-finite values.
Results may differ from the reference program's by a relative error of at most 0.0003.
Values sent between devices are 32-bit elements; how exact they have to be, the bound alone decides.
A program may use at most 128 MiB of HBM per device.

```python
import math
import jax
import jax.numpy as jnp
import numpy as np
from jax import lax

D = 4096
FF = 14336
VOCAB = 128256
PROJ = 64
LEN = 256
SEQS = 64
TOKENS = 16384
QUERIES = 32


def place_ends(values, key, least, high):
    longest = values.shape.index(max(values.shape))
    spots = []
    for shift in (0, 1):
        where = [jax.random.randint(jax.random.fold_in(key, axis), (), 0, length) for axis, length in enumerate(values.shape)]
        where[longest] = (where[longest] + shift) % values.shape[longest]
        spots.append(tuple(where))
    return values.at[spots[0]].set(least).at[spots[1]].set(high)


def block_scale(stream_key, dims, shards, low, top_value):
    gain, own = 1.0, jax.random.fold_in(stream_key, 6)
    for axis_at, blocks in shards:
        steps = jnp.exp(jax.random.uniform(jax.random.fold_in(own, axis_at), (blocks,), jnp.float32, low / len(shards), top_value / len(shards)))
        gain = gain * jnp.repeat(steps, dims[axis_at] // blocks).reshape([-1 if axis == axis_at else 1 for axis in range(len(dims))])
    return gain


def skewed_wide(stream_key, shape, count, slope):
    loads = [min(1 << octave, count + 1 - (1 << octave)) * (1 << 20) // math.isqrt((1 << octave) ** slope) + 1 for octave in range((count + 1).bit_length()) if 1 << octave <= count]
    deviation = 1 + sum(loads) // (1 << 30)
    grid = np.cumsum(np.array([max(1, weight // deviation) for weight in loads]))
    ticket = jax.random.randint(jax.random.fold_in(stream_key, 1), shape, 0, int(grid[len(loads) - 1]))
    start = jnp.left_shift(1, jnp.searchsorted(jnp.asarray(grid, jnp.int32), ticket, side="right").astype(jnp.int32))
    rank = start - 1 + jax.random.randint(jax.random.fold_in(stream_key, 4), shape, 0, 1 << 30) % jnp.minimum(start, count + 1 - start)
    return jax.random.permutation(jax.random.fold_in(stream_key, 2), count)[rank].astype(jnp.int32)


def gaussian(key, extent, spread, bound, cuts=(), kind=jnp.bfloat16):
    loudness = block_scale(key, extent, cuts, -0.22, 0.18) if cuts else 1.0
    drawn = jax.random.normal(key, extent, jnp.float32) * spread * loudness
    return jnp.minimum(jnp.maximum(drawn, -bound), bound).astype(kind)


def setup_inputs(seed: int = 0, part: int = 0) -> dict:
    key_of = jax.random.split(jax.random.key(seed), 8)
    own_keys = jax.random.split(jax.random.fold_in(key_of[7], part), 8)
    in_acts = gaussian(own_keys[0], (TOKENS, D), 1.0, 6.0, ((0, 4), (1, 4)))
    out_grad = gaussian(own_keys[1], (TOKENS, FF), 1.0, 6.0, ((0, 4), (1, 4)))
    proj_in = gaussian(key_of[2], (D, PROJ), D ** -0.5, 0.09375, ((0, 4),))
    proj_out = gaussian(key_of[3], (FF, PROJ), FF ** -0.5, 0.046875, ((0, 4),))
    token_ids = place_ends(skewed_wide(own_keys[4], (SEQS, LEN), VOCAB, 2), jax.random.fold_in(own_keys[4], 3), 0, VOCAB - 1).astype(jnp.int32)
    token_weight = jnp.clip(jnp.exp(jax.random.uniform(key_of[5], (VOCAB,), jnp.float32, math.log(0.25), math.log(4.0))), 0.25, 4.0)
    query_ids = place_ends(jax.random.randint(own_keys[6], (QUERIES,), 0, SEQS), jax.random.fold_in(own_keys[6], 1), 0, SEQS - 1).astype(jnp.int32)
    return dict(in_acts=in_acts, out_grad=out_grad, proj_in=proj_in, proj_out=proj_out, token_ids=token_ids, token_weight=token_weight, query_ids=query_ids)


def precondition(seq_grads, fisher_in, fisher_out):
    width = seq_grads.shape[1]
    count = seq_grads.shape[0]
    trace_value = jnp.trace(fisher_in)
    identity = jnp.eye(width, dtype=jnp.float32)
    chol_in = jnp.linalg.cholesky(fisher_in + 0.1 * trace_value / width * identity)
    chol_out = jnp.linalg.cholesky(fisher_out + 0.1 * trace_value / width * identity)
    stacked = seq_grads.transpose(1, 0, 2).reshape(width, count * width)
    solved_left = jax.scipy.linalg.cho_solve((chol_out, True), stacked).reshape(width, count, width)
    turned = solved_left.transpose(2, 1, 0).reshape(width, count * width)
    solved_both = jax.scipy.linalg.cho_solve((chol_in, True), turned).reshape(width, count, width)
    return solved_both.transpose(1, 2, 0) * (trace_value / width)

def reference(in_acts, out_grad, proj_in, proj_out, token_ids, token_weight, query_ids):
    seq_total, length = token_ids.shape
    width = proj_in.shape[1]
    x_proj = jnp.dot(in_acts.astype(jnp.float32), proj_in.astype(jnp.float32), preferred_element_type=jnp.float32)
    weights = jnp.take(token_weight, token_ids.reshape(-1), axis=0)
    g_proj = jnp.dot(out_grad.astype(jnp.float32), proj_out.astype(jnp.float32), preferred_element_type=jnp.float32) * weights[:, None]
    x_seq = x_proj.reshape(seq_total, length, width)
    g_seq = g_proj.reshape(seq_total, length, width)
    seq_grads = jnp.einsum('nlr,nlc->nrc', g_seq, x_seq, precision=lax.Precision.HIGHEST)
    fisher_in = jnp.einsum('nrc,nrd->cd', seq_grads, seq_grads, precision=lax.Precision.HIGHEST) / seq_total
    fisher_out = jnp.einsum('nrc,ndc->rd', seq_grads, seq_grads, precision=lax.Precision.HIGHEST) / seq_total
    precond = precondition(seq_grads, fisher_in, fisher_out)
    chosen = jnp.take(precond, query_ids, axis=0)
    scores = jnp.einsum('qrc,nrc->qn', chosen, seq_grads, precision=lax.Precision.HIGHEST)
    return (seq_grads, scores)
```

```python
import functools

import jax
import jax.numpy as jnp
from jax import lax
from jax.experimental import pallas as pl
from jax.experimental.pallas import tpu as pltpu
from jax.sharding import PartitionSpec as P

MESH = pl.DeviceIdType.MESH
F32 = jnp.float32
BF16 = jnp.bfloat16
EXACT = lax.Precision.HIGHEST
CHUNK = 128
LAG = 3


def contract(a, b, a_dim, b_dim, precision=EXACT):
    return lax.dot_general(
        a, b, (((a_dim,), (b_dim,)), ((), ())), precision=precision, preferred_element_type=F32
    )


def invert_pair(first, second):
    width = first.shape[0]
    lane = lax.broadcasted_iota(jnp.int32, (1, 2 * width), 1) % width
    row_of = lax.broadcasted_iota(jnp.int32, (width, 2 * width), 0)

    def pivot(a, j):
        row, col = a[j : j + 1, :], a[:, j : j + 1]
        inverse = 1.0 / a[j : j + 1, j : j + 1]
        scaled = jnp.where(lane == j, inverse, row * inverse)
        updated = jnp.where(lane == j, 0.0, a) - col * scaled
        return jnp.where(row_of == j, scaled, updated)

    def turn(a):
        a = jnp.concatenate([a[8:, :], a[:8, :]], axis=0)
        return pltpu.roll(a, 2 * width - 8, 1)

    def block(_, pair):
        a, b = pair
        for j in range(8):
            a, b = pivot(a, j), pivot(b, j)
        return turn(a), turn(b)

    return lax.fori_loop(0, width // 8, block, (first, second))


def kernel(
    hids, exs, rounds, seq_total,
    acts, grads, proj_in, proj_out, ids, table, queries,
    rows_out, scores_out,
    acts_v, grads_v, proj_x, proj_g, table_v, own, came, seq, seq_flat, seq_cut, pre_cut, fish,
    seq_all, pre_all, rows_in, partial, parts_in,
    load_sem, hop_send, hop_recv, fish_send, fish_recv, seq_send, seq_recv,
    row_send, row_recv, pre_send, pre_recv, part_send, part_recv,
):
    hid, ex = lax.axis_index("hid"), lax.axis_index("ex")
    width = proj_in.shape[1]
    half = rounds * CHUNK
    owners = 2 * exs
    mine = seq.shape[0]
    row_count = width // hids
    cut = width // owners

    def loads(k):
        copies = []
        for side in range(2):
            place = pl.ds(side * half + k * CHUNK, CHUNK)
            land = pl.ds(k * 2 * CHUNK + side * CHUNK, CHUNK)
            copies.append(pltpu.make_async_copy(acts.at[place], acts_v.at[land], load_sem.at[side, k]))
            copies.append(pltpu.make_async_copy(grads.at[place], grads_v.at[land], load_sem.at[2 + side, k]))
        return copies

    def start_loads(k, _):
        for copy in loads(k):
            copy.start()
        return 0

    lax.fori_loop(0, rounds, start_loads, 0)

    barrier = pltpu.get_barrier_semaphore()
    for dh in range(hids):
        for de in range(exs):
            if dh or de:
                pl.semaphore_signal(
                    barrier, inc=1, device_id={"hid": (hid + dh) % hids, "ex": (ex + de) % exs}, device_id_type=MESH
                )

    proj_x[...] = jnp.concatenate([proj_in[...], jnp.zeros_like(proj_in[...])], axis=1)
    proj_g[...] = jnp.concatenate([jnp.zeros_like(proj_out[...]), proj_out[...]], axis=1)
    high = table[...].astype(BF16)
    table_v[:, :128] = high
    table_v[:, 128:] = (table[...] - high.astype(F32)).astype(BF16)
    seq[...] = jnp.zeros_like(seq)
    pl.semaphore_wait(barrier, hids * exs - 1)

    def hop(side, k):
        return pltpu.make_async_remote_copy(
            src_ref=own.at[side, k],
            dst_ref=came.at[side, k],
            send_sem=hop_send.at[side, k],
            recv_sem=hop_recv.at[side, k],
            device_id={"hid": (hid + 2 * side - 1 + hids) % hids},
            device_id_type=MESH,
        )

    def weight_row(at):
        token = ids[pl.ds(at, 1), :]
        row_of = lax.broadcasted_iota(jnp.int32, (table.shape[0], CHUNK), 0)
        hot = jnp.where(row_of == token // 128, 1.0, 0.0).astype(BF16)
        picked = contract(table_v[...], hot, 0, 0, None)
        picked = picked[:128] + picked[128:]
        lane_of = lax.broadcasted_iota(jnp.int32, (128, CHUNK), 0)
        return jnp.sum(jnp.where(lane_of == token % 128, picked, 0.0), axis=0, keepdims=True)

    def relay(side, r):
        steps = side * hid + (1 - side) * (hids - 1 - hid)
        k = r - LAG * steps
        live = (k >= 0) & (k < rounds)

        @pl.when(live & (steps > 0) & (steps < hids - 1))
        def _():
            hop(side, k).wait_recv()
            own[side, k] = own[side, k] + came[side, k]

        @pl.when(live & (steps < hids - 1))
        def _():
            hop(side, k).start()

        @pl.when(live & (steps == hids - 1))
        def _():
            weight = weight_row(side * rounds + k)
            hop(side, k).wait_recv()
            both = own[side, k] + came[side, k]
            product = contract(both.T * weight, both, 1, 0)
            n = k * CHUNK // (half // mine)
            seq[n] = seq[n] + product[width:, :width]

    first = 1 - hid * 2 // hids

    def round_of(r, _):
        @pl.when(r < rounds)
        def _():
            for copy in loads(r):
                copy.wait()
            place = pl.ds(r * 2 * CHUNK, 2 * CHUNK)
            both = jnp.dot(acts_v[place, :], proj_x[...], preferred_element_type=F32)
            both = both + jnp.dot(grads_v[place, :], proj_g[...], preferred_element_type=F32)
            own[0, r] = both[:CHUNK]
            own[1, r] = both[CHUNK:]

        relay(first, r)
        relay(1 - first, r)
        return 0

    lax.fori_loop(0, rounds + LAG * (hids - 1), round_of, 0)

    def sent(k, _):
        for side in range(2):
            @pl.when(hid != side * (hids - 1))
            def _():
                hop(side, k).wait_send()
        return 0

    lax.fori_loop(0, rounds, sent, 0)

    ends = (hid == 0) | (hid == hids - 1)
    side = hid // (hids - 1)
    me = ex * 2 + side

    def to_owner(source, target, send, recv, step, indexed):
        other = (me + step) % owners
        return pltpu.make_async_remote_copy(
            src_ref=source.at[other] if indexed else source.at[me],
            dst_ref=target.at[me],
            send_sem=send.at[other],
            recv_sem=recv.at[me],
            device_id={"hid": other % 2 * (hids - 1), "ex": other // 2},
            device_id_type=MESH,
        )

    def from_owner(target, recv, step):
        other = (me + step) % owners
        return pltpu.make_async_copy(target.at[other], target.at[other], recv.at[other])

    def row_copy(step):
        other = (hid + step) % hids
        return pltpu.make_async_remote_copy(
            src_ref=seq.at[:, pl.ds(other * row_count, row_count), :],
            dst_ref=rows_in.at[side],
            send_sem=row_send.at[other],
            recv_sem=row_recv.at[side],
            device_id={"hid": other},
            device_id_type=MESH,
        )

    def part_copy(dh, de):
        other_hid, other_ex = (hid + dh) % hids, (ex + de) % exs
        return pltpu.make_async_remote_copy(
            src_ref=partial.at[other_ex],
            dst_ref=parts_in.at[me],
            send_sem=part_send.at[other_hid * exs + other_ex],
            recv_sem=part_recv.at[me],
            device_id={"hid": other_hid, "ex": other_ex},
            device_id_type=MESH,
        )

    others = [(dh, de) for de in range(exs) for dh in range(hids) if dh or de]

    @pl.when(ends)
    def _():
        all_rows = seq[...].reshape(mine * width, width)
        seq_flat[...] = all_rows
        in_part = contract(all_rows, all_rows, 0, 0)
        out_part = jnp.zeros((width, width), F32)
        for n in range(mine):
            out_part = out_part + contract(seq[n], seq[n], 1, 1)
        fish[me] = jnp.concatenate([in_part, out_part], axis=1)
        for step in range(1, owners):
            to_owner(fish, fish, fish_send, fish_recv, step, False).start()
        for n in range(mine):
            for o in range(owners):
                seq_cut[o, n * cut : (n + 1) * cut, :] = seq[n, o * cut : (o + 1) * cut, :]
        seq_all[me] = seq_cut[me]
        for step in range(1, owners):
            to_owner(seq_cut, seq_all, seq_send, seq_recv, step, True).start()
        for step in range(1, hids):
            row_copy(step).start()
        rows_in[side] = seq[:, pl.ds(hid * row_count, row_count), :]

        for step in range(1, owners):
            from_owner(fish, fish_recv, step).wait()
        fisher = jnp.sum(fish[...], axis=0) * (1.0 / seq_total)
        row_of = lax.broadcasted_iota(jnp.int32, (width, 2 * width), 0)
        lane_of = lax.broadcasted_iota(jnp.int32, (width, 2 * width), 1)
        trace = jnp.sum(jnp.where(row_of == lane_of, fisher, 0.0), axis=(0, 1), keepdims=True)
        swapped = pltpu.roll(fisher, width, 1)
        damp = jnp.where(row_of == lane_of % width, 0.1 * trace / width, 0.0)
        in_inverse, out_inverse = invert_pair(
            jnp.where(lane_of < width, fisher, swapped) + damp,
            jnp.where(lane_of < width, swapped, fisher) + damp,
        )
        in_inverse = in_inverse[:, :width]
        out_inverse = out_inverse[:, :width] * (trace / width)
        right = contract(seq_flat[...], in_inverse, 1, 0)
        for n in range(mine):
            left = contract(out_inverse, right[n * width : (n + 1) * width], 1, 0)
            for o in range(owners):
                pre_cut[o, n * cut : (n + 1) * cut, :] = left[o * cut : (o + 1) * cut]
        for step in range(1, owners):
            to_owner(pre_cut, pre_all, pre_send, pre_recv, step, True).start()
        pre_all[me] = pre_cut[me]
        for step in range(1, owners):
            from_owner(seq_all, seq_recv, step).wait()
            from_owner(pre_all, pre_recv, step).wait()
        total = owners * mine
        gram = jnp.zeros((total, total), F32)
        pre_flat = pre_all.reshape(total * cut, width)
        seq_rows = seq_all.reshape(total * cut, width)
        for row in range(cut):
            picked = pl.ds(row, total, stride=cut)
            gram = gram + contract(pre_flat[picked, :], seq_rows[picked, :], 1, 1)
        hot = jnp.where(
            lax.broadcasted_iota(jnp.int32, (total, queries.shape[1]), 0) == queries[...], 1.0, 0.0
        )
        chosen = contract(gram, hot, 0, 0)
        for e in range(exs):
            partial[e] = chosen[e * 2 * mine : (e + 1) * 2 * mine]
        for dh, de in others:
            part_copy(dh, de).start()
        parts_in[me] = partial[ex]

    for s in range(2):
        @pl.when(hid != s * (hids - 1))
        def _():
            pltpu.make_async_copy(rows_in.at[s], rows_in.at[s], row_recv.at[s]).wait()
    rows_out[...] = rows_in[...].reshape(rows_out.shape)
    for o in range(owners):
        @pl.when((hid != o % 2 * (hids - 1)) | (ex != o // 2))
        def _():
            pltpu.make_async_copy(parts_in.at[o], parts_in.at[o], part_recv.at[o]).wait()
    scores_out[...] = jnp.sum(parts_in[...], axis=0)

    @pl.when(ends)
    def _():
        for step in range(1, owners):
            to_owner(fish, fish, fish_send, fish_recv, step, False).wait_send()
            to_owner(seq_cut, seq_all, seq_send, seq_recv, step, True).wait_send()
            to_owner(pre_cut, pre_all, pre_send, pre_recv, step, True).wait_send()
        for step in range(1, hids):
            row_copy(step).wait_send()
        for dh, de in others:
            part_copy(dh, de).wait_send()


def fused(hids, exs, in_acts, out_grad, proj_in, proj_out, token_ids, token_weight, query_ids):
    seq_count, length = token_ids.shape
    width = proj_in.shape[1]
    tokens, depth = in_acts.shape
    wide = out_grad.shape[1]
    rounds = tokens // 2 // CHUNK
    mine = seq_count // 2
    owners = 2 * exs
    cut = width // owners
    row_count = width // hids
    count = query_ids.shape[0]
    table_rows = -(-token_weight.shape[0] // 2048) * 16
    table = jnp.pad(token_weight, (0, table_rows * 128 - token_weight.shape[0])).reshape(table_rows, 128)
    vmem = pl.BlockSpec(memory_space=pltpu.VMEM)
    whole = pl.BlockSpec(memory_space=pl.ANY)
    sem = pltpu.SemaphoreType.DMA
    rows, scores = pl.pallas_call(
        functools.partial(kernel, hids, exs, rounds, seq_count * exs),
        out_shape=(
            jax.ShapeDtypeStruct((seq_count, row_count, width), F32),
            jax.ShapeDtypeStruct((seq_count, count), F32),
        ),
        in_specs=[whole, whole] + [vmem] * 5,
        out_specs=(vmem, vmem),
        scratch_shapes=[
            pltpu.VMEM((tokens, depth), BF16),
            pltpu.VMEM((tokens, wide), BF16),
            pltpu.VMEM((depth, 2 * width), BF16),
            pltpu.VMEM((wide, 2 * width), BF16),
            pltpu.VMEM((table_rows, 256), BF16),
            pltpu.VMEM((2, rounds, CHUNK, 2 * width), F32),
            pltpu.VMEM((2, rounds, CHUNK, 2 * width), F32),
            pltpu.VMEM((mine, width, width), F32),
            pltpu.VMEM((mine * width, width), F32),
            pltpu.VMEM((owners, mine * cut, width), F32),
            pltpu.VMEM((owners, mine * cut, width), F32),
            pltpu.VMEM((owners, width, 2 * width), F32),
            pltpu.VMEM((owners, mine * cut, width), F32),
            pltpu.VMEM((owners, mine * cut, width), F32),
            pltpu.VMEM((2, mine, row_count, width), F32),
            pltpu.VMEM((exs, 2 * mine, count), F32),
            pltpu.VMEM((owners, 2 * mine, count), F32),
            sem((4, rounds)),
            sem((2, rounds)),
            sem((2, rounds)),
            sem((owners,)),
            sem((owners,)),
            sem((owners,)),
            sem((owners,)),
            sem((hids,)),
            sem((2,)),
            sem((owners,)),
            sem((owners,)),
            sem((hids * exs,)),
            sem((owners,)),
        ],
        compiler_params=pltpu.CompilerParams(
            collective_id=0, has_side_effects=True, vmem_limit_bytes=60 * 1024 * 1024
        ),
        cost_estimate=pl.CostEstimate(
            flops=4 * tokens * (depth + wide) * width, bytes_accessed=2 * tokens * (depth + wide), transcendentals=0
        ),
    )(
        in_acts,
        out_grad,
        proj_in,
        proj_out,
        token_ids.reshape(tokens // CHUNK, CHUNK),
        table,
        query_ids.reshape(1, count),
    )
    return rows, scores.T


def precondition(seq_grads, fisher_in, fisher_out):
    width = seq_grads.shape[1]
    count = seq_grads.shape[0]
    trace_value = jnp.trace(fisher_in)
    identity = jnp.eye(width, dtype=jnp.float32)
    chol_in = jnp.linalg.cholesky(fisher_in + 0.1 * trace_value / width * identity)
    chol_out = jnp.linalg.cholesky(fisher_out + 0.1 * trace_value / width * identity)
    stacked = seq_grads.transpose(1, 0, 2).reshape(width, count * width)
    solved_left = jax.scipy.linalg.cho_solve((chol_out, True), stacked).reshape(width, count, width)
    turned = solved_left.transpose(2, 1, 0).reshape(width, count * width)
    solved_both = jax.scipy.linalg.cho_solve((chol_in, True), turned).reshape(width, count, width)
    return solved_both.transpose(1, 2, 0) * (trace_value / width)


def shards(in_acts, out_grad, proj_in, proj_out, token_ids, token_weight, query_ids):
    seq_count, length = token_ids.shape
    width = proj_in.shape[1]
    hid_count = lax.axis_size("hid")
    row_count = width // hid_count
    row_start = lax.axis_index("hid") * row_count
    x_part = jnp.dot(in_acts, proj_in, preferred_element_type=jnp.float32)
    weights = jnp.take(token_weight, token_ids.reshape(-1), axis=0)
    g_part = jnp.dot(out_grad, proj_out, preferred_element_type=jnp.float32) * weights[:, None]
    x_proj, g_proj = lax.psum((x_part, g_part), "hid")
    seq_grads = jnp.einsum(
        "nlr,nlc->nrc",
        g_proj.reshape(seq_count, length, width),
        x_proj.reshape(seq_count, length, width),
        precision=lax.Precision.HIGHEST,
    )
    own_rows = lax.dynamic_slice_in_dim(seq_grads, row_start, row_count, 1)
    seq_total = seq_count * lax.axis_size("ex")
    in_part = jnp.einsum("nrc,nrd->cd", seq_grads, seq_grads, precision=lax.Precision.HIGHEST)
    out_part = jnp.einsum("nrc,ndc->rd", seq_grads, seq_grads, precision=lax.Precision.HIGHEST)
    fisher_in, fisher_out = lax.psum((in_part, out_part), "ex")
    precond = precondition(seq_grads, fisher_in / seq_total, fisher_out / seq_total)
    gathered = lax.all_gather(precond, "ex", axis=0, tiled=True)
    chosen = jnp.take(gathered, query_ids, axis=0)
    scores = jnp.einsum("qrc,nrc->qn", chosen, seq_grads, precision=lax.Precision.HIGHEST)
    return (own_rows, scores)


def solution(mesh):
    hids, exs = mesh.shape["hid"], mesh.shape["ex"]
    fits = hids > 1 and 64 % (8 * hids) == 0 and 64 % (16 * exs) == 0
    body = functools.partial(fused, hids, exs) if fits else shards
    placed = (
        P(("grp", "ex"), "hid"),
        P(("grp", "ex"), "hid"),
        P("hid", None),
        P("hid", None),
        P(("grp", "ex"), None),
        P(),
        P("grp"),
    )
    return jax.shard_map(
        body,
        mesh=mesh,
        in_specs=placed,
        out_specs=(P(("grp", "ex"), "hid", None), P("grp", "ex")),
        check_vma=False,
    )
```

```python
import functools

import jax
import jax.numpy as jnp
from jax import lax
from jax.experimental import pallas as pl
from jax.experimental.pallas import tpu as pltpu
from jax.sharding import PartitionSpec as P

MESH = pl.DeviceIdType.MESH
F32 = jnp.float32
BF16 = jnp.bfloat16
EXACT = lax.Precision.HIGHEST
CHUNK = 128
LAG = 3
AHEAD = 3


def contract(a, b, a_dim, b_dim, precision=EXACT):
    return lax.dot_general(
        a, b, (((a_dim,), (b_dim,)), ((), ())), precision=precision, preferred_element_type=F32
    )


def invert_pair(first, second):
    width = first.shape[0]
    lane = lax.broadcasted_iota(jnp.int32, (1, 2 * width), 1) % width
    row_of = lax.broadcasted_iota(jnp.int32, (width, 2 * width), 0)

    def pivot(a, j):
        row, col = a[j : j + 1, :], a[:, j : j + 1]
        inverse = 1.0 / a[j : j + 1, j : j + 1]
        scaled = jnp.where(lane == j, inverse, row * inverse)
        updated = jnp.where(lane == j, 0.0, a) - col * scaled
        return jnp.where(row_of == j, scaled, updated)

    def turn(a):
        a = jnp.concatenate([a[8:, :], a[:8, :]], axis=0)
        return pltpu.roll(a, 2 * width - 8, 1)

    def block(_, pair):
        a, b = pair
        for j in range(8):
            a, b = pivot(a, j), pivot(b, j)
        return turn(a), turn(b)

    return lax.fori_loop(0, width // 8, block, (first, second))


def kernel(
    hids, exs, rounds, seq_total,
    acts, grads, proj_in_hbm, proj_out_hbm, ids, table_hbm, queries,
    rows_out, scores_out,
    acts_v, grads_v, proj_in, proj_out, table, table_v, own, came, seq, seq_cut, pre_cut, fish,
    seq_all, pre_all, rows_in, partial, parts_in,
    small_sem, load_sem, hop_send, hop_recv, fish_send, fish_recv, seq_send, seq_recv,
    row_send, row_recv, pre_send, pre_recv, part_send, part_recv,
):
    hid, ex = lax.axis_index("hid"), lax.axis_index("ex")
    width = proj_in.shape[0]
    half = rounds * CHUNK
    owners = 2 * exs
    mine = seq.shape[0]
    row_count = width // hids
    cut = width // owners
    ends = (hid == 0) | (hid == hids - 1)
    side = hid // (hids - 1)
    me = ex * 2 + side

    small = [
        pltpu.make_async_copy(source, target, small_sem.at[i])
        for i, (source, target) in enumerate(((proj_in_hbm, proj_in), (proj_out_hbm, proj_out), (table_hbm, table)))
    ]

    def loads(k):
        copies = []
        for side in range(2):
            place = pl.ds(side * half + k * CHUNK, CHUNK)
            land = pl.ds(k * 2 * CHUNK + side * CHUNK, CHUNK)
            copies.append(pltpu.make_async_copy(acts.at[place], acts_v.at[land], load_sem.at[side, k]))
            copies.append(pltpu.make_async_copy(grads.at[place], grads_v.at[land], load_sem.at[2 + side, k]))
        return copies

    def start_loads(k, _):
        for copy in loads(k):
            copy.start()
        return 0

    barrier = pltpu.get_barrier_semaphore()
    for dh in range(hids):
        for de in range(exs):
            if dh or de:
                pl.semaphore_signal(
                    barrier, inc=1, device_id={"hid": (hid + dh) % hids, "ex": (ex + de) % exs}, device_id_type=MESH
                )

    for copy in small:
        copy.start()
    lax.fori_loop(0, min(AHEAD, rounds), start_loads, 0)
    for copy in small:
        copy.wait()
    high = table[...].astype(BF16)
    table_v[:, :128] = high
    table_v[:, 128:] = (table[...] - high.astype(F32)).astype(BF16)
    seq[...] = jnp.zeros_like(seq)
    fish[me] = jnp.zeros((width, 2 * width), F32)
    pl.semaphore_wait(barrier, hids * exs - 1)

    def hop(side, k):
        return pltpu.make_async_remote_copy(
            src_ref=own.at[side, k],
            dst_ref=came.at[side, k],
            send_sem=hop_send.at[side, k],
            recv_sem=hop_recv.at[side, k],
            device_id={"hid": (hid + 2 * side - 1 + hids) % hids},
            device_id_type=MESH,
        )

    def weight_row(side, k):
        per_seq = ids.shape[1] // CHUNK
        row = ids[pl.ds(side * mine + k // per_seq, 1), :]
        token = row[:, :CHUNK]
        for piece in range(1, per_seq):
            token = jnp.where(k % per_seq == piece, row[:, piece * CHUNK : (piece + 1) * CHUNK], token)
        row_of = lax.broadcasted_iota(jnp.int32, (table.shape[0], CHUNK), 0)
        hot = jnp.where(row_of == token // 128, 1.0, 0.0).astype(BF16)
        picked = contract(table_v[...], hot, 0, 0, None)
        picked = picked[:128] + picked[128:]
        lane_of = lax.broadcasted_iota(jnp.int32, (128, CHUNK), 0)
        return jnp.sum(jnp.where(lane_of == token % 128, picked, 0.0), axis=0, keepdims=True)

    def relay(side, r):
        steps = side * hid + (1 - side) * (hids - 1 - hid)
        k = r - LAG * steps
        live = (k >= 0) & (k < rounds)

        @pl.when(live & (steps > 0) & (steps < hids - 1))
        def _():
            hop(side, k).wait_recv()
            own[side, k] = own[side, k] + came[side, k]

        @pl.when(live & (steps < hids - 1))
        def _():
            hop(side, k).start()

        @pl.when(live & (steps == hids - 1))
        def _():
            weight = weight_row(side, k)
            hop(side, k).wait_recv()
            both = own[side, k] + came[side, k]
            per_seq = ids.shape[1] // CHUNK
            n = k // per_seq
            seq[n] = seq[n] + contract(both[width:] * weight, both[:width], 1, 1)

            @pl.when(k % per_seq == per_seq - 1)
            def _():
                done = seq[n]
                sides = [contract(done, done, 0, 0), contract(done, done, 1, 1)]
                fish[me] = fish[me] + jnp.concatenate(sides, axis=1)
                for o in range(owners):
                    seq_cut[o, pl.ds(pl.multiple_of(n * cut, cut), cut), :] = done[o * cut : (o + 1) * cut]

    first = 1 - hid * 2 // hids

    def round_of(r, _):
        @pl.when(r < rounds)
        def _():
            for copy in loads(r):
                copy.wait()

            @pl.when(r + AHEAD < rounds)
            def _():
                start_loads(r + AHEAD, 0)

            place = pl.ds(r * 2 * CHUNK, 2 * CHUNK)
            x_part = contract(proj_in[...], acts_v[place, :], 1, 1, None)
            g_part = contract(proj_out[...], grads_v[place, :], 1, 1, None)
            for side in range(2):
                own[side, r, :width] = x_part[:, side * CHUNK : (side + 1) * CHUNK]
                own[side, r, width:] = g_part[:, side * CHUNK : (side + 1) * CHUNK]

        relay(first, r)
        relay(1 - first, r)
        return 0

    lax.fori_loop(0, rounds + LAG * (hids - 1), round_of, 0)

    def sent(k, _):
        for side in range(2):
            @pl.when(hid != side * (hids - 1))
            def _():
                hop(side, k).wait_send()
        return 0


    def to_owner(source, target, send, recv, step, indexed):
        other = (me + step) % owners
        return pltpu.make_async_remote_copy(
            src_ref=source.at[other] if indexed else source.at[me],
            dst_ref=target.at[me],
            send_sem=send.at[other],
            recv_sem=recv.at[me],
            device_id={"hid": other % 2 * (hids - 1), "ex": other // 2},
            device_id_type=MESH,
        )

    def from_owner(target, recv, step):
        other = (me + step) % owners
        return pltpu.make_async_copy(target.at[other], target.at[other], recv.at[other])

    def row_copy(step):
        other = (hid + step) % hids
        return pltpu.make_async_remote_copy(
            src_ref=seq.at[:, pl.ds(other * row_count, row_count), :],
            dst_ref=rows_in.at[side],
            send_sem=row_send.at[other],
            recv_sem=row_recv.at[side],
            device_id={"hid": other},
            device_id_type=MESH,
        )

    def part_copy(dh, de):
        other_hid, other_ex = (hid + dh) % hids, (ex + de) % exs
        return pltpu.make_async_remote_copy(
            src_ref=partial.at[other_ex],
            dst_ref=parts_in.at[me],
            send_sem=part_send.at[other_hid * exs + other_ex],
            recv_sem=part_recv.at[me],
            device_id={"hid": other_hid, "ex": other_ex},
            device_id_type=MESH,
        )

    others = [(dh, de) for dh in range(hids - 1, -1, -1) for de in range(exs) if dh or de]
    partners = [*range(1, owners, 2), *range(2, owners, 2)]

    @pl.when(ends)
    def _():
        for step in partners:
            to_owner(fish, fish, fish_send, fish_recv, step, False).start()
        for step in partners:
            from_owner(fish, fish_recv, step).wait()
        seq_all[me] = seq_cut[me]
        for step in partners:
            to_owner(seq_cut, seq_all, seq_send, seq_recv, step, True).start()
        for step in range(1, hids):
            row_copy(step).start()
        rows_in[side] = seq[:, pl.ds(hid * row_count, row_count), :]

        fisher = jnp.sum(fish[...], axis=0) * (1.0 / seq_total)
        row_of = lax.broadcasted_iota(jnp.int32, (width, 2 * width), 0)
        lane_of = lax.broadcasted_iota(jnp.int32, (width, 2 * width), 1)
        trace = jnp.sum(jnp.where(row_of == lane_of, fisher, 0.0), axis=(0, 1), keepdims=True)
        swapped = pltpu.roll(fisher, width, 1)
        damp = jnp.where(row_of == lane_of % width, 0.1 * trace / width, 0.0)
        in_inverse, out_inverse = invert_pair(
            jnp.where(lane_of < width, fisher, swapped) + damp,
            jnp.where(lane_of < width, swapped, fisher) + damp,
        )
        in_inverse = in_inverse[:, :width]
        out_inverse = out_inverse[:, :width] * (trace / width)
        right = contract(seq[...].reshape(mine * width, width), in_inverse, 1, 0)
        for n in range(mine):
            left = contract(out_inverse, right[n * width : (n + 1) * width], 1, 0)
            for o in range(owners):
                pre_cut[o, n * cut : (n + 1) * cut, :] = left[o * cut : (o + 1) * cut]
        for step in partners:
            to_owner(pre_cut, pre_all, pre_send, pre_recv, step, True).start()
        pre_all[me] = pre_cut[me]
        for step in partners:
            from_owner(seq_all, seq_recv, step).wait()
            from_owner(pre_all, pre_recv, step).wait()
        total = owners * mine
        gram = jnp.zeros((total, total), F32)
        pre_flat = pre_all.reshape(total * cut, width)
        seq_rows = seq_all.reshape(total * cut, width)
        for row in range(cut):
            picked = pl.ds(row, total, stride=cut)
            gram = gram + contract(pre_flat[picked, :], seq_rows[picked, :], 1, 1)
        hot = jnp.where(
            lax.broadcasted_iota(jnp.int32, (total, queries.shape[1]), 0) == queries[...], 1.0, 0.0
        )
        chosen = contract(gram, hot, 0, 0)
        for e in range(exs):
            partial[e] = chosen[e * 2 * mine : (e + 1) * 2 * mine]
        for dh, de in others:
            part_copy(dh, de).start()
        parts_in[me] = partial[ex]

    for s in range(2):
        @pl.when(hid != s * (hids - 1))
        def _():
            pltpu.make_async_copy(rows_in.at[s], rows_in.at[s], row_recv.at[s]).wait()
    rows_out[...] = rows_in[...].reshape(rows_out.shape)
    for o in range(owners):
        @pl.when((hid != o % 2 * (hids - 1)) | (ex != o // 2))
        def _():
            pltpu.make_async_copy(parts_in.at[o], parts_in.at[o], part_recv.at[o]).wait()
    scores_out[...] = jnp.sum(parts_in[...], axis=0)

    lax.fori_loop(0, rounds, sent, 0)

    @pl.when(ends)
    def _():
        for step in range(1, owners):
            to_owner(fish, fish, fish_send, fish_recv, step, False).wait_send()
            to_owner(seq_cut, seq_all, seq_send, seq_recv, step, True).wait_send()
            to_owner(pre_cut, pre_all, pre_send, pre_recv, step, True).wait_send()
        for step in range(1, hids):
            row_copy(step).wait_send()
        for dh, de in others:
            part_copy(dh, de).wait_send()


def fused(hids, exs, in_acts, out_grad, proj_in, proj_out, token_ids, token_weight, query_ids):
    seq_count, length = token_ids.shape
    width = proj_in.shape[1]
    tokens, depth = in_acts.shape
    wide = out_grad.shape[1]
    rounds = tokens // 2 // CHUNK
    mine = seq_count // 2
    owners = 2 * exs
    cut = width // owners
    row_count = width // hids
    count = query_ids.shape[0]
    table_rows = token_weight.shape[0] // 128
    vmem = pl.BlockSpec(memory_space=pltpu.VMEM)
    whole = pl.BlockSpec(memory_space=pl.ANY)
    sem = pltpu.SemaphoreType.DMA
    rows, scores = pl.pallas_call(
        functools.partial(kernel, hids, exs, rounds, seq_count * exs),
        out_shape=(
            jax.ShapeDtypeStruct((seq_count, row_count, width), F32),
            jax.ShapeDtypeStruct((seq_count, count), F32),
        ),
        in_specs=[whole, whole, whole, whole, vmem, whole, vmem],
        out_specs=(vmem, vmem),
        scratch_shapes=[
            pltpu.VMEM((tokens, depth), BF16),
            pltpu.VMEM((tokens, wide), BF16),
            pltpu.VMEM((width, depth), BF16),
            pltpu.VMEM((width, wide), BF16),
            pltpu.VMEM((table_rows, 128), F32),
            pltpu.VMEM((table_rows, 256), BF16),
            pltpu.VMEM((2, rounds, 2 * width, CHUNK), F32),
            pltpu.VMEM((2, rounds, 2 * width, CHUNK), F32),
            pltpu.VMEM((mine, width, width), F32),
            pltpu.VMEM((owners, mine * cut, width), F32),
            pltpu.VMEM((owners, mine * cut, width), F32),
            pltpu.VMEM((owners, width, 2 * width), F32),
            pltpu.VMEM((owners, mine * cut, width), F32),
            pltpu.VMEM((owners, mine * cut, width), F32),
            pltpu.VMEM((2, mine, row_count, width), F32),
            pltpu.VMEM((exs, 2 * mine, count), F32),
            pltpu.VMEM((owners, 2 * mine, count), F32),
            sem((3,)),
            sem((4, rounds)),
            sem((2, rounds)),
            sem((2, rounds)),
            sem((owners,)),
            sem((owners,)),
            sem((owners,)),
            sem((owners,)),
            sem((hids,)),
            sem((2,)),
            sem((owners,)),
            sem((owners,)),
            sem((hids * exs,)),
            sem((owners,)),
        ],
        compiler_params=pltpu.CompilerParams(
            collective_id=0, has_side_effects=True, vmem_limit_bytes=60 * 1024 * 1024
        ),
        cost_estimate=pl.CostEstimate(
            flops=4 * tokens * (depth + wide) * width, bytes_accessed=2 * tokens * (depth + wide), transcendentals=0
        ),
    )(
        in_acts,
        out_grad,
        proj_in.T,
        proj_out.T,
        token_ids,
        token_weight.reshape(table_rows, 128),
        query_ids.reshape(1, count),
    )
    return rows, scores.T


def precondition(seq_grads, fisher_in, fisher_out):
    width = seq_grads.shape[1]
    count = seq_grads.shape[0]
    trace_value = jnp.trace(fisher_in)
    identity = jnp.eye(width, dtype=jnp.float32)
    chol_in = jnp.linalg.cholesky(fisher_in + 0.1 * trace_value / width * identity)
    chol_out = jnp.linalg.cholesky(fisher_out + 0.1 * trace_value / width * identity)
    stacked = seq_grads.transpose(1, 0, 2).reshape(width, count * width)
    solved_left = jax.scipy.linalg.cho_solve((chol_out, True), stacked).reshape(width, count, width)
    turned = solved_left.transpose(2, 1, 0).reshape(width, count * width)
    solved_both = jax.scipy.linalg.cho_solve((chol_in, True), turned).reshape(width, count, width)
    return solved_both.transpose(1, 2, 0) * (trace_value / width)


def shards(in_acts, out_grad, proj_in, proj_out, token_ids, token_weight, query_ids):
    seq_count, length = token_ids.shape
    width = proj_in.shape[1]
    hid_count = lax.axis_size("hid")
    row_count = width // hid_count
    row_start = lax.axis_index("hid") * row_count
    x_part = jnp.dot(in_acts, proj_in, preferred_element_type=jnp.float32)
    weights = jnp.take(token_weight, token_ids.reshape(-1), axis=0)
    g_part = jnp.dot(out_grad, proj_out, preferred_element_type=jnp.float32) * weights[:, None]
    x_proj, g_proj = lax.psum((x_part, g_part), "hid")
    seq_grads = jnp.einsum(
        "nlr,nlc->nrc",
        g_proj.reshape(seq_count, length, width),
        x_proj.reshape(seq_count, length, width),
        precision=lax.Precision.HIGHEST,
    )
    own_rows = lax.dynamic_slice_in_dim(seq_grads, row_start, row_count, 1)
    seq_total = seq_count * lax.axis_size("ex")
    in_part = jnp.einsum("nrc,nrd->cd", seq_grads, seq_grads, precision=lax.Precision.HIGHEST)
    out_part = jnp.einsum("nrc,ndc->rd", seq_grads, seq_grads, precision=lax.Precision.HIGHEST)
    fisher_in, fisher_out = lax.psum((in_part, out_part), "ex")
    precond = precondition(seq_grads, fisher_in / seq_total, fisher_out / seq_total)
    gathered = lax.all_gather(precond, "ex", axis=0, tiled=True)
    chosen = jnp.take(gathered, query_ids, axis=0)
    scores = jnp.einsum("qrc,nrc->qn", chosen, seq_grads, precision=lax.Precision.HIGHEST)
    return (own_rows, scores)


def solution(mesh):
    hids, exs = mesh.shape["hid"], mesh.shape["ex"]
    fits = hids > 1 and 64 % (8 * hids) == 0 and 64 % (16 * exs) == 0
    body = functools.partial(fused, hids, exs) if fits else shards
    placed = (
        P(("grp", "ex"), "hid"),
        P(("grp", "ex"), "hid"),
        P("hid", None),
        P("hid", None),
        P(("grp", "ex"), None),
        P(),
        P("grp"),
    )
    return jax.shard_map(
        body,
        mesh=mesh,
        in_specs=placed,
        out_specs=(P(("grp", "ex"), "hid", None), P("grp", "ex")),
        check_vma=False,
    )
```

```python
import functools

import jax
import jax.numpy as jnp
from jax import lax
from jax.experimental import pallas as pl
from jax.experimental.pallas import tpu as pltpu
from jax.sharding import PartitionSpec as P

MESH = pl.DeviceIdType.MESH
F32 = jnp.float32
BF16 = jnp.bfloat16
EXACT = lax.Precision.HIGHEST
CHUNK = 128
LAG = 3
LATE = 4
AHEAD = 3


def contract(a, b, a_dim, b_dim, precision=EXACT):
    return lax.dot_general(
        a, b, (((a_dim,), (b_dim,)), ((), ())), precision=precision, preferred_element_type=F32
    )


def invert_pair(first, second):
    width = first.shape[0]
    lane = lax.broadcasted_iota(jnp.int32, (1, 2 * width), 1) % width
    row_of = lax.broadcasted_iota(jnp.int32, (width, 2 * width), 0)

    def pivot(a, j):
        row, col = a[j : j + 1, :], a[:, j : j + 1]
        inverse = 1.0 / a[j : j + 1, j : j + 1]
        scaled = jnp.where(lane == j, inverse, row * inverse)
        updated = jnp.where(lane == j, 0.0, a) - col * scaled
        return jnp.where(row_of == j, scaled, updated)

    def turn(a):
        a = jnp.concatenate([a[8:, :], a[:8, :]], axis=0)
        return pltpu.roll(a, 2 * width - 8, 1)

    def block(_, pair):
        a, b = pair
        for j in range(8):
            a, b = pivot(a, j), pivot(b, j)
        return turn(a), turn(b)

    return lax.fori_loop(0, width // 8, block, (first, second))


def kernel(
    hids, exs, rounds, seq_total,
    acts, grads, proj_in_hbm, proj_out_hbm, ids, table_hbm, queries,
    rows_out, scores_out,
    acts_v, grads_v, proj_in, proj_out, table, table_v, own, came, seq, seq_cut, pre_cut, fish,
    seq_all, pre_all, rows_in, partial, parts_in,
    small_sem, load_sem, hop_send, hop_recv, fish_send, fish_recv, seq_send, seq_recv,
    row_send, row_recv, pre_send, pre_recv, part_send, part_recv,
):
    hid, ex = lax.axis_index("hid"), lax.axis_index("ex")
    width = proj_in.shape[0]
    half = rounds * CHUNK
    owners = 2 * exs
    mine = seq.shape[0]
    row_count = width // hids
    cut = width // owners
    ends = (hid == 0) | (hid == hids - 1)
    side = hid // (hids - 1)
    me = ex * 2 + side

    small = [
        pltpu.make_async_copy(source, target, small_sem.at[i])
        for i, (source, target) in enumerate(((proj_in_hbm, proj_in), (proj_out_hbm, proj_out), (table_hbm, table)))
    ]

    def loads(k):
        copies = []
        for side in range(2):
            place = pl.ds(side * half + k * CHUNK, CHUNK)
            land = pl.ds(k * 2 * CHUNK + side * CHUNK, CHUNK)
            copies.append(pltpu.make_async_copy(acts.at[place], acts_v.at[land], load_sem.at[side, k]))
            copies.append(pltpu.make_async_copy(grads.at[place], grads_v.at[land], load_sem.at[2 + side, k]))
        return copies

    def start_loads(k, _):
        for copy in loads(k):
            copy.start()
        return 0

    barrier = pltpu.get_barrier_semaphore()
    for dh in range(hids):
        for de in range(exs):
            if dh or de:
                pl.semaphore_signal(
                    barrier, inc=1, device_id={"hid": (hid + dh) % hids, "ex": (ex + de) % exs}, device_id_type=MESH
                )

    for copy in small:
        copy.start()
    lax.fori_loop(0, min(AHEAD, rounds), start_loads, 0)
    for copy in small:
        copy.wait()
    high = table[...].astype(BF16)
    table_v[:, :128] = high
    table_v[:, 128:] = (table[...] - high.astype(F32)).astype(BF16)
    seq[...] = jnp.zeros_like(seq)
    fish[me] = jnp.zeros((width, 2 * width), F32)
    pl.semaphore_wait(barrier, hids * exs - 1)

    def hop(side, k):
        return pltpu.make_async_remote_copy(
            src_ref=own.at[side, k],
            dst_ref=came.at[side, k],
            send_sem=hop_send.at[side, k],
            recv_sem=hop_recv.at[side, k],
            device_id={"hid": (hid + 2 * side - 1 + hids) % hids},
            device_id_type=MESH,
        )

    def weight_row(side, k):
        per_seq = ids.shape[1] // CHUNK
        row = ids[pl.ds(side * mine + k // per_seq, 1), :]
        token = row[:, :CHUNK]
        for piece in range(1, per_seq):
            token = jnp.where(k % per_seq == piece, row[:, piece * CHUNK : (piece + 1) * CHUNK], token)
        row_of = lax.broadcasted_iota(jnp.int32, (table.shape[0], CHUNK), 0)
        hot = jnp.where(row_of == token // 128, 1.0, 0.0).astype(BF16)
        picked = contract(table_v[...], hot, 0, 0, None)
        picked = picked[:128] + picked[128:]
        lane_of = lax.broadcasted_iota(jnp.int32, (128, CHUNK), 0)
        return jnp.sum(jnp.where(lane_of == token % 128, picked, 0.0), axis=0, keepdims=True)

    def relay(side, r):
        steps = side * hid + (1 - side) * (hids - 1 - hid)
        k = r - LAG * steps - LATE * (steps // (hids - 1))
        live = (k >= 0) & (k < rounds)

        @pl.when(live & (steps > 0) & (steps < hids - 1))
        def _():
            hop(side, k).wait_recv()
            own[side, k] = own[side, k] + came[side, k]

        @pl.when(live & (steps < hids - 1))
        def _():
            hop(side, k).start()

        @pl.when(live & (steps == hids - 1))
        def _():
            weight = weight_row(side, k)
            hop(side, k).wait_recv()
            both = own[side, k] + came[side, k]
            per_seq = ids.shape[1] // CHUNK
            n = k // per_seq
            seq[n] = seq[n] + contract(both[width:] * weight, both[:width], 1, 1)

            @pl.when(k % per_seq == per_seq - 1)
            def _():
                done = seq[n]
                sides = [contract(done, done, 0, 0), contract(done, done, 1, 1)]
                fish[me] = fish[me] + jnp.concatenate(sides, axis=1)
                for o in range(owners):
                    seq_cut[o, pl.ds(pl.multiple_of(n * cut, cut), cut), :] = done[o * cut : (o + 1) * cut]

    first = 1 - hid * 2 // hids

    def round_of(r, _):
        @pl.when(r < rounds)
        def _():
            for copy in loads(r):
                copy.wait()

            @pl.when(r + AHEAD < rounds)
            def _():
                start_loads(r + AHEAD, 0)

            place = pl.ds(r * 2 * CHUNK, 2 * CHUNK)
            x_part = contract(proj_in[...], acts_v[place, :], 1, 1, None)
            g_part = contract(proj_out[...], grads_v[place, :], 1, 1, None)
            for side in range(2):
                own[side, r, :width] = x_part[:, side * CHUNK : (side + 1) * CHUNK]
                own[side, r, width:] = g_part[:, side * CHUNK : (side + 1) * CHUNK]

        relay(first, r)
        relay(1 - first, r)
        return 0

    lax.fori_loop(0, rounds + LAG * (hids - 1) + LATE, round_of, 0)

    def sent(k, _):
        for side in range(2):
            @pl.when(hid != side * (hids - 1))
            def _():
                hop(side, k).wait_send()
        return 0


    def to_owner(source, target, send, recv, step, indexed):
        other = (me + step) % owners
        return pltpu.make_async_remote_copy(
            src_ref=source.at[other] if indexed else source.at[me],
            dst_ref=target.at[me],
            send_sem=send.at[other],
            recv_sem=recv.at[me],
            device_id={"hid": other % 2 * (hids - 1), "ex": other // 2},
            device_id_type=MESH,
        )

    def from_owner(target, recv, step):
        other = (me + step) % owners
        return pltpu.make_async_copy(target.at[other], target.at[other], recv.at[other])

    def row_copy(step):
        other = (hid + step) % hids
        return pltpu.make_async_remote_copy(
            src_ref=seq.at[:, pl.ds(other * row_count, row_count), :],
            dst_ref=rows_in.at[side],
            send_sem=row_send.at[other],
            recv_sem=row_recv.at[side],
            device_id={"hid": other},
            device_id_type=MESH,
        )

    def part_copy(dh, de):
        other_hid, other_ex = (hid + dh) % hids, (ex + de) % exs
        return pltpu.make_async_remote_copy(
            src_ref=partial.at[other_ex],
            dst_ref=parts_in.at[me],
            send_sem=part_send.at[other_hid * exs + other_ex],
            recv_sem=part_recv.at[me],
            device_id={"hid": other_hid, "ex": other_ex},
            device_id_type=MESH,
        )

    others = [(dh, de) for dh in range(hids - 1, -1, -1) for de in range(exs) if dh or de]
    partners = [*range(1, owners, 2), *range(2, owners, 2)]

    @pl.when(ends)
    def _():
        for step in partners:
            to_owner(fish, fish, fish_send, fish_recv, step, False).start()
        for step in partners:
            from_owner(fish, fish_recv, step).wait()
        seq_all[me] = seq_cut[me]
        for step in partners:
            to_owner(seq_cut, seq_all, seq_send, seq_recv, step, True).start()
        for step in range(1, hids):
            row_copy(step).start()
        rows_in[side] = seq[:, pl.ds(hid * row_count, row_count), :]

        fisher = jnp.sum(fish[...], axis=0) * (1.0 / seq_total)
        row_of = lax.broadcasted_iota(jnp.int32, (width, 2 * width), 0)
        lane_of = lax.broadcasted_iota(jnp.int32, (width, 2 * width), 1)
        trace = jnp.sum(jnp.where(row_of == lane_of, fisher, 0.0), axis=(0, 1), keepdims=True)
        swapped = pltpu.roll(fisher, width, 1)
        damp = jnp.where(row_of == lane_of % width, 0.1 * trace / width, 0.0)
        in_inverse, out_inverse = invert_pair(
            jnp.where(lane_of < width, fisher, swapped) + damp,
            jnp.where(lane_of < width, swapped, fisher) + damp,
        )
        in_inverse = in_inverse[:, :width]
        out_inverse = out_inverse[:, :width] * (trace / width)
        right = contract(seq[...].reshape(mine * width, width), in_inverse, 1, 0)
        for n in range(mine):
            left = contract(out_inverse, right[n * width : (n + 1) * width], 1, 0)
            for o in range(owners):
                pre_cut[o, n * cut : (n + 1) * cut, :] = left[o * cut : (o + 1) * cut]
        for step in partners:
            to_owner(pre_cut, pre_all, pre_send, pre_recv, step, True).start()
        pre_all[me] = pre_cut[me]
        for step in partners:
            from_owner(seq_all, seq_recv, step).wait()
            from_owner(pre_all, pre_recv, step).wait()
        total = owners * mine
        gram = jnp.zeros((total, total), F32)
        pre_flat = pre_all.reshape(total * cut, width)
        seq_rows = seq_all.reshape(total * cut, width)
        for row in range(cut):
            picked = pl.ds(row, total, stride=cut)
            gram = gram + contract(pre_flat[picked, :], seq_rows[picked, :], 1, 1)
        hot = jnp.where(
            lax.broadcasted_iota(jnp.int32, (total, queries.shape[1]), 0) == queries[...], 1.0, 0.0
        )
        chosen = contract(gram, hot, 0, 0)
        for e in range(exs):
            partial[e] = chosen[e * 2 * mine : (e + 1) * 2 * mine]
        for dh, de in others:
            part_copy(dh, de).start()
        parts_in[me] = partial[ex]

    for s in range(2):
        @pl.when(hid != s * (hids - 1))
        def _():
            pltpu.make_async_copy(rows_in.at[s], rows_in.at[s], row_recv.at[s]).wait()
    rows_out[...] = rows_in[...]
    for o in range(owners):
        @pl.when((hid != o % 2 * (hids - 1)) | (ex != o // 2))
        def _():
            pltpu.make_async_copy(parts_in.at[o], parts_in.at[o], part_recv.at[o]).wait()
    scores_out[...] = parts_in[...]

    lax.fori_loop(0, rounds, sent, 0)

    @pl.when(ends)
    def _():
        for step in range(1, owners):
            to_owner(fish, fish, fish_send, fish_recv, step, False).wait_send()
            to_owner(seq_cut, seq_all, seq_send, seq_recv, step, True).wait_send()
            to_owner(pre_cut, pre_all, pre_send, pre_recv, step, True).wait_send()
        for step in range(1, hids):
            row_copy(step).wait_send()
        for dh, de in others:
            part_copy(dh, de).wait_send()


def finish(rows, parts, rows_out, scores_out):
    rows_out[...] = rows[...].reshape(rows_out.shape)
    scores_out[...] = jnp.sum(parts[...], axis=0).T


def fused(hids, exs, in_acts, out_grad, proj_in, proj_out, token_ids, token_weight, query_ids):
    seq_count, length = token_ids.shape
    width = proj_in.shape[1]
    tokens, depth = in_acts.shape
    wide = out_grad.shape[1]
    rounds = tokens // 2 // CHUNK
    mine = seq_count // 2
    owners = 2 * exs
    cut = width // owners
    row_count = width // hids
    count = query_ids.shape[0]
    table_rows = token_weight.shape[0] // 128
    vmem = pl.BlockSpec(memory_space=pltpu.VMEM)
    whole = pl.BlockSpec(memory_space=pl.ANY)
    sem = pltpu.SemaphoreType.DMA
    rows, parts = pl.pallas_call(
        functools.partial(kernel, hids, exs, rounds, seq_count * exs),
        out_shape=(
            jax.ShapeDtypeStruct((2, mine, row_count, width), F32),
            jax.ShapeDtypeStruct((owners, seq_count, count), F32),
        ),
        in_specs=[whole, whole, whole, whole, vmem, whole, vmem],
        out_specs=(vmem, vmem),
        scratch_shapes=[
            pltpu.VMEM((tokens, depth), BF16),
            pltpu.VMEM((tokens, wide), BF16),
            pltpu.VMEM((width, depth), BF16),
            pltpu.VMEM((width, wide), BF16),
            pltpu.VMEM((table_rows, 128), F32),
            pltpu.VMEM((table_rows, 256), BF16),
            pltpu.VMEM((2, rounds, 2 * width, CHUNK), F32),
            pltpu.VMEM((2, rounds, 2 * width, CHUNK), F32),
            pltpu.VMEM((mine, width, width), F32),
            pltpu.VMEM((owners, mine * cut, width), F32),
            pltpu.VMEM((owners, mine * cut, width), F32),
            pltpu.VMEM((owners, width, 2 * width), F32),
            pltpu.VMEM((owners, mine * cut, width), F32),
            pltpu.VMEM((owners, mine * cut, width), F32),
            pltpu.VMEM((2, mine, row_count, width), F32),
            pltpu.VMEM((exs, 2 * mine, count), F32),
            pltpu.VMEM((owners, 2 * mine, count), F32),
            sem((3,)),
            sem((4, rounds)),
            sem((2, rounds)),
            sem((2, rounds)),
            sem((owners,)),
            sem((owners,)),
            sem((owners,)),
            sem((owners,)),
            sem((hids,)),
            sem((2,)),
            sem((owners,)),
            sem((owners,)),
            sem((hids * exs,)),
            sem((owners,)),
        ],
        compiler_params=pltpu.CompilerParams(
            collective_id=0, has_side_effects=True, vmem_limit_bytes=60 * 1024 * 1024
        ),
        cost_estimate=pl.CostEstimate(
            flops=4 * tokens * (depth + wide) * width, bytes_accessed=2 * tokens * (depth + wide), transcendentals=0
        ),
    )(
        in_acts,
        out_grad,
        proj_in.T,
        proj_out.T,
        token_ids,
        token_weight.reshape(table_rows, 128),
        query_ids.reshape(1, count),
    )
    return pl.pallas_call(
        finish,
        out_shape=(
            jax.ShapeDtypeStruct((seq_count, row_count, width), F32),
            jax.ShapeDtypeStruct((count, seq_count), F32),
        ),
        in_specs=[vmem, vmem],
        out_specs=(vmem, vmem),
    )(rows, parts)


def precondition(seq_grads, fisher_in, fisher_out):
    width = seq_grads.shape[1]
    count = seq_grads.shape[0]
    trace_value = jnp.trace(fisher_in)
    identity = jnp.eye(width, dtype=jnp.float32)
    chol_in = jnp.linalg.cholesky(fisher_in + 0.1 * trace_value / width * identity)
    chol_out = jnp.linalg.cholesky(fisher_out + 0.1 * trace_value / width * identity)
    stacked = seq_grads.transpose(1, 0, 2).reshape(width, count * width)
    solved_left = jax.scipy.linalg.cho_solve((chol_out, True), stacked).reshape(width, count, width)
    turned = solved_left.transpose(2, 1, 0).reshape(width, count * width)
    solved_both = jax.scipy.linalg.cho_solve((chol_in, True), turned).reshape(width, count, width)
    return solved_both.transpose(1, 2, 0) * (trace_value / width)


def shards(in_acts, out_grad, proj_in, proj_out, token_ids, token_weight, query_ids):
    seq_count, length = token_ids.shape
    width = proj_in.shape[1]
    hid_count = lax.axis_size("hid")
    row_count = width // hid_count
    row_start = lax.axis_index("hid") * row_count
    x_part = jnp.dot(in_acts, proj_in, preferred_element_type=jnp.float32)
    weights = jnp.take(token_weight, token_ids.reshape(-1), axis=0)
    g_part = jnp.dot(out_grad, proj_out, preferred_element_type=jnp.float32) * weights[:, None]
    x_proj, g_proj = lax.psum((x_part, g_part), "hid")
    seq_grads = jnp.einsum(
        "nlr,nlc->nrc",
        g_proj.reshape(seq_count, length, width),
        x_proj.reshape(seq_count, length, width),
        precision=lax.Precision.HIGHEST,
    )
    own_rows = lax.dynamic_slice_in_dim(seq_grads, row_start, row_count, 1)
    seq_total = seq_count * lax.axis_size("ex")
    in_part = jnp.einsum("nrc,nrd->cd", seq_grads, seq_grads, precision=lax.Precision.HIGHEST)
    out_part = jnp.einsum("nrc,ndc->rd", seq_grads, seq_grads, precision=lax.Precision.HIGHEST)
    fisher_in, fisher_out = lax.psum((in_part, out_part), "ex")
    precond = precondition(seq_grads, fisher_in / seq_total, fisher_out / seq_total)
    gathered = lax.all_gather(precond, "ex", axis=0, tiled=True)
    chosen = jnp.take(gathered, query_ids, axis=0)
    scores = jnp.einsum("qrc,nrc->qn", chosen, seq_grads, precision=lax.Precision.HIGHEST)
    return (own_rows, scores)


def solution(mesh):
    hids, exs = mesh.shape["hid"], mesh.shape["ex"]
    fits = hids > 1 and 64 % (8 * hids) == 0 and 64 % (16 * exs) == 0
    body = functools.partial(fused, hids, exs) if fits else shards
    placed = (
        P(("grp", "ex"), "hid"),
        P(("grp", "ex"), "hid"),
        P("hid", None),
        P("hid", None),
        P(("grp", "ex"), None),
        P(),
        P("grp"),
    )
    return jax.shard_map(
        body,
        mesh=mesh,
        in_specs=placed,
        out_specs=(P(("grp", "ex"), "hid", None), P("grp", "ex")),
        check_vma=False,
    )
```
